32 devices in a mesh: wa: 8 (over y, x, core), ha: 4 (over z).
Axes of the slice: x: 2, y: 2, z: 4, core: 2. Of those that a mesh axis runs over, the one named last changes fastest.
Arguments:
- residual_in: bfloat16 [48, 16384], P('ha', 'wa'), may hold values from -43.25 to 43.25
- grad_out: bfloat16 [48, 16384], P('ha', 'wa'), may hold values from -6 to 6
- norm_gain: bfloat16 [16384], P('wa'), may hold values from 0.099609375 to 1.8984375
- w_gate: bfloat16 [16384, 26624], P('wa', 'ha'), may hold values from -0.0390625 to 0.0390625
- w_up: bfloat16 [16384, 26624], P('wa', 'ha'), may hold values from -0.0390625 to 0.0390625
- w_down: bfloat16 [26624, 16384], P('ha', 'wa'), may hold values from -0.030643146 to 0.030643146
Outputs:
- grad_in: bfloat16 [48, 16384], P('ha', 'wa')
The draws below stay inside these ranges and needn't reach their ends.
All inputs are finite; a program needn't handle non-finite values.
Results may differ from the reference program's by a relative error of at most 0.0053.
Values may be sent and summed in bfloat16 or wider, within the bound.
A program may use at most 128 MiB of HBM per device.

```python
import jax
import jax.numpy as jnp
from jax import lax

D = 16384
FF = 26624
TOKENS = 48


def draw_residual_in(key, part):
    key_rows, key_cols, key_base = jax.random.split(key, 3)
    row_scale = jnp.exp(jax.random.uniform(key_rows, (TOKENS, 1), jnp.float32) * jnp.log(10.0))
    col_rand = jnp.exp(jax.random.uniform(key_cols, (1, D), jnp.float32) * jnp.log(10.0))
    ramp = jnp.arange(D, dtype=jnp.float32)[None, :] / (D - 1)
    col_scale = col_rand * (1.0 + 0.8 * ramp)
    base = jnp.clip(jax.random.normal(key_base, (TOKENS, D), jnp.float32), -4.0, 4.0)
    return (0.06 * base * row_scale * col_scale).astype(jnp.bfloat16)


def draw_w_gate(key, part):
    shared_key = jax.random.fold_in(key, 101)
    shared = jax.random.normal(shared_key, (D, FF), jnp.float32)
    return (jnp.clip(shared, -5.0, 5.0) * D ** (-0.5)).astype(jnp.bfloat16)


def draw_w_up(key, part):
    shared_key = jax.random.fold_in(key, 101)
    own_key = jax.random.fold_in(key, 102)
    shared = jax.random.normal(shared_key, (D, FF), jnp.float32)
    own = jax.random.normal(own_key, (D, FF), jnp.float32)
    mixed = 0.7 * shared + 0.714 * own
    return (jnp.clip(mixed, -5.0, 5.0) * D ** (-0.5)).astype(jnp.bfloat16)


def draw_w_down(key, part):
    own_key = jax.random.fold_in(key, 201)
    row_key = jax.random.fold_in(key, 202)
    own = jax.random.normal(own_key, (FF, D), jnp.float32)
    common_row = jax.random.normal(row_key, (1, D), jnp.float32)
    mixed = own + 0.6 * common_row
    return (jnp.clip(mixed, -5.0, 5.0) * FF ** (-0.5)).astype(jnp.bfloat16)


def levels(key, dims, cuts, low, high):
    loudness, own = 1.0, jax.random.fold_in(key, 6)
    for dim, shards_of in cuts:
        draws = jnp.exp(jax.random.uniform(jax.random.fold_in(own, dim), (shards_of,), jnp.float32, low / len(cuts), high / len(cuts)))
        loudness = loudness * jnp.repeat(draws, dims[dim] // shards_of).reshape([-1 if axis == dim else 1 for axis in range(len(dims))])
    return loudness


def noise(key, extent, spread, limit, cuts=(), kind=jnp.bfloat16):
    drawn = spread * jax.random.normal(key, extent, jnp.float32)
    if cuts:
        drawn = drawn * levels(key, extent, cuts, -0.22, 0.18)
    return jnp.clip(drawn, -limit, limit).astype(kind)


def setup_inputs(seed: int = 0) -> dict:
    key_list = jax.random.split(jax.random.key(seed), 7)
    return {
        "residual_in": draw_residual_in(jax.random.fold_in(key_list[6], 71), 0),
        "grad_out": noise(key_list[1], (TOKENS, D), 1.0, 6.0, ((0, 4), (1, 8))),
        "norm_gain": jnp.clip(1.0 + 0.18 * jax.random.normal(key_list[2], (D,), jnp.float32), 0.099609375, 1.8984375).astype(jnp.bfloat16),
        "w_gate": draw_w_gate(jax.random.fold_in(key_list[6], 71), 0),
        "w_up": draw_w_up(jax.random.fold_in(key_list[6], 71), 0),
        "w_down": draw_w_down(jax.random.fold_in(key_list[6], 71), 0),
    }


def reference(residual_in, grad_out, norm_gain, w_gate, w_up, w_down):
    stream = residual_in.astype(jnp.float32)
    inv_rms = lax.rsqrt(lax.optimization_barrier(jnp.mean(stream * stream, axis=1, keepdims=True)) + 1e-05)
    gain_f = norm_gain.astype(jnp.float32)
    normed = (stream * inv_rms * gain_f).astype(jnp.bfloat16)
    gate = jnp.dot(normed, w_gate, preferred_element_type=jnp.float32)
    up = jnp.dot(normed, w_up, preferred_element_type=jnp.float32)
    d_hidden = jnp.dot(grad_out, w_down.T, preferred_element_type=jnp.float32)
    sig = jax.nn.sigmoid(gate)
    d_up = (d_hidden * gate * sig).astype(jnp.bfloat16)
    d_gate = (d_hidden * up * sig * (1.0 + gate * (1.0 - sig))).astype(jnp.bfloat16)
    d_normed = jnp.dot(d_gate, w_gate.T, preferred_element_type=jnp.float32)
    d_normed = d_normed + jnp.dot(d_up, w_up.T, preferred_element_type=jnp.float32)
    scaled = d_normed * gain_f
    row_dot = lax.optimization_barrier(jnp.sum(scaled * stream, axis=1, keepdims=True))
    grad_in = grad_out.astype(jnp.float32) + inv_rms * scaled - stream * inv_rms ** 3 * row_dot / D
    return grad_in.astype(jnp.bfloat16)
```

```python
import functools

import jax
import jax.numpy as jnp
from jax import lax
from jax.experimental import pallas as pl
from jax.experimental.pallas import tpu as pltpu
from jax.sharding import PartitionSpec as P

MESH = pl.DeviceIdType.MESH
D = 16384
CHUNKS = 13
SLOTS = 4
DEEP = 8
DEEP_DOWN = 6
F32, BF16 = jnp.float32, jnp.bfloat16
NT = (((1,), (1,)), ((), ()))


def fused(n_wa, n_ha, res, go, gain, wg, wu, wd, out,
          wgs, wus, wds, xb, tmp, xf, gf, xs, gos, sq, sq_in, inv_half, inv_own,
          part, pair_in, rs_out, rs_in, gb, acc, rd, rd_in, rz, rz_in, own, fs, fr, tail,
          g_sem, u_sem, d_sem, x_ss, x_rs, sq_ss, sq_rs, p_ss, p_rs, r_ss, r_rs,
          a_ss, a_rs, f_ss, f_rs, rd_ss, rd_rs, rz_ss, rz_rs, t_ss, t_rs):
    me, z = lax.axis_index("wa"), lax.axis_index("ha")
    chip, core = me // 2, me % 2
    n_chip = n_wa // 2
    r, width = res.shape
    rows, half, wide, cols4 = r * n_ha, r * n_ha // 2, width // 2, width // 4
    ch = wg.shape[1] // CHUNKS
    sub = ch // n_chip

    def columns(c):
        return pl.ds(pl.multiple_of(c * ch, ch), ch)

    def load_g(c):
        return pltpu.make_async_copy(wg.at[:, columns(c)], wgs.at[c % DEEP], g_sem.at[c % DEEP])

    def load_u(c):
        return pltpu.make_async_copy(wu.at[:, columns(c)], wus.at[c % DEEP], u_sem.at[c % DEEP])

    def load_d(c):
        return pltpu.make_async_copy(wd.at[columns(c), :], wds.at[c % DEEP_DOWN], d_sem.at[c % DEEP_DOWN])

    def remote(src, dst, ss, rs, wa, ha):
        return pltpu.make_async_remote_copy(
            src_ref=src, dst_ref=dst, send_sem=ss, recv_sem=rs,
            device_id=(wa, ha), device_id_type=MESH)

    def peer_chip(d):
        return (chip ^ d) * 2 + core

    for c in range(min(DEEP, CHUNKS)):
        load_g(c).start()
        load_u(c).start()
        if c < DEEP_DOWN:
            load_d(c).start()

    barrier = pltpu.get_barrier_semaphore()
    for d in range(1, n_ha):
        pl.semaphore_signal(barrier, inc=1, device_id=(me, z ^ d), device_id_type=MESH)
    for d in range(1, n_wa):
        pl.semaphore_signal(barrier, inc=1, device_id=(me ^ d, z), device_id_type=MESH)

    for j, ref in enumerate((res, go)):
        for h in range(2):
            at = (2 * j + h) * r
            tmp[at:at + r, :] = ref[:, h * wide:(h + 1) * wide].astype(F32)
    xb[z] = tmp[...].astype(BF16)
    pl.semaphore_wait(barrier, n_ha + n_wa - 2)

    def gather(d):
        return remote(xb.at[z], xb.at[z], x_ss.at[d - 1], x_rs.at[d - 1], me, z ^ d)

    for d in range(1, n_ha):
        gather(d).start()
    acc[...] = jnp.zeros_like(acc)
    rd[...] = jnp.zeros_like(rd)
    rz[...] = jnp.zeros_like(rz)
    for d in range(1, n_ha):
        gather(d).wait()
    for k in range(n_ha):
        tmp[...] = xb[k].astype(F32)
        for j, ref in enumerate((xf, gf)):
            for h in range(2):
                at = (2 * j + h) * r
                ref[k * r:(k + 1) * r, h * wide:(h + 1) * wide] = tmp[at:at + r, :]
    x = xf[...]
    xs[...] = (x * gain[...]).astype(BF16)
    gos[...] = gf[...].astype(BF16)
    lanes = x[:, 0:128] * x[:, 0:128]
    for j in range(1, width // 128):
        piece = x[:, j * 128:(j + 1) * 128]
        lanes = lanes + piece * piece
    sq[...] = lanes

    def squares(d):
        return remote(sq, sq_in.at[d - 1], sq_ss.at[d - 1], sq_rs.at[d - 1], me ^ d, z)

    for d in range(1, n_wa):
        squares(d).start()

    def pair(c):
        s = c % SLOTS
        return remote(part.at[s, 1 - core], pair_in.at[s], p_ss.at[s], p_rs.at[s], me ^ 1, z)

    def scatter(c, d):
        s = c % SLOTS
        return remote(rs_out.at[s, chip ^ d], rs_in.at[s, d - 1], r_ss.at[s, d - 1], r_rs.at[s, d - 1],
                      peer_chip(d), z)

    def spread(c, d):
        s = c % SLOTS
        return remote(gb.at[c, core, chip], gb.at[c, core, chip], a_ss.at[s, d - 1], a_rs.at[s, d - 1],
                      peer_chip(d), z)

    def forward(c):
        s = c % SLOTS
        return remote(gb.at[c, core], gb.at[c, core], f_ss.at[s], f_rs.at[s], me ^ 1, z)

    def share_rd(d):
        return remote(rd, rd_in.at[d - 1], rd_ss.at[d - 1], rd_rs.at[d - 1], me ^ d, z)

    def step(i, carry):
        @pl.when(i < CHUNKS)
        def _():
            s = i % SLOTS
            load_g(i).wait()
            load_u(i).wait()
            load_d(i).wait()
            a = xs[...]
            gate = jnp.dot(a, wgs[i % DEEP], preferred_element_type=F32)
            up = jnp.dot(a, wus[i % DEEP], preferred_element_type=F32)
            back = lax.dot_general(gos[...], wds[i % DEEP_DOWN], NT, preferred_element_type=F32)
            for h in range(2):
                for j, v in enumerate((gate, up, back)):
                    part[s, h, j * half:(j + 1) * half, :] = v[h * half:(h + 1) * half, :]
            pair(i).start()

            @pl.when(i + DEEP_DOWN < CHUNKS)
            def _():
                load_d(i + DEEP_DOWN).start()

        @pl.when((i >= 1) & (i < CHUNKS + 1))
        def _():
            c = i - 1
            s = c % SLOTS
            pair(c).wait()
            both = part[s, core] + pair_in[s]
            for k in range(n_chip):
                rs_out[s, k] = both[:, k * sub:(k + 1) * sub]
            for d in range(1, n_chip):
                scatter(c, d).start()

        @pl.when(i == 2)
        def _():
            for d in range(1, n_wa):
                squares(d).wait()
            total = sq[...]
            for d in range(1, n_wa):
                total = total + sq_in[d - 1]
            inv = lax.rsqrt(jnp.sum(total, axis=1, keepdims=True) / D + 1e-05)
            wide_inv = jnp.broadcast_to(inv, (rows, 128))
            for h in range(2):
                inv_half[h] = wide_inv[h * half:(h + 1) * half, :]
            xf[:, 0:128] = wide_inv
            for k in range(n_ha):
                inv_own[k] = xf[k * r:(k + 1) * r, 0:128]

        @pl.when((i >= 2) & (i < CHUNKS + 2))
        def _():
            c = i - 2
            s = c % SLOTS
            for d in range(1, n_chip):
                scatter(c, d).wait()
            total = rs_out[s, chip]
            for d in range(1, n_chip):
                total = total + rs_in[s, d - 1]
            inv = inv_half[core][:, 0:1]
            gate, up, d_hidden = total[:half] * inv, total[half:2 * half] * inv, total[2 * half:]
            sig = jax.nn.sigmoid(gate)
            d_up = d_hidden * gate * sig
            d_gate = d_hidden * up * sig * (1.0 + gate * (1.0 - sig))
            stacked = jnp.concatenate([d_gate, d_up], axis=0).astype(BF16)
            gb[c, core, chip] = stacked
            for d in range(1, n_chip):
                spread(c, d).start()
            kept = stacked.astype(F32)
            terms = kept[:half] * gate + kept[half:] * up
            for j in range(sub // 128):
                rd[...] += terms[:, j * 128:(j + 1) * 128]

        @pl.when(i == CHUNKS + 1)
        def _():
            for d in range(1, n_wa):
                share_rd(d).start()

        @pl.when((i >= 3) & (i < CHUNKS + 3))
        def _():
            c = i - 3
            for d in range(1, n_chip):
                spread(c, d).wait()
            forward(c).start()

        @pl.when(i >= 4)
        def _():
            c = i - 4
            s = c % DEEP
            forward(c).wait()
            halves = [
                jnp.concatenate([gb[c, h, k] for k in range(n_chip)], axis=1).astype(F32)
                for h in range(2)
            ]
            d_gate = jnp.concatenate([v[:half] for v in halves], axis=0).astype(BF16)
            d_up = jnp.concatenate([v[half:] for v in halves], axis=0).astype(BF16)
            for j in range(4):
                at = slice(j * cols4, (j + 1) * cols4)
                acc[:, at] += lax.dot_general(
                    d_gate, wgs[s, at, :], NT, preferred_element_type=F32
                ) + lax.dot_general(d_up, wus[s, at, :], NT, preferred_element_type=F32)

            @pl.when(c + DEEP < CHUNKS)
            def _():
                load_g(c + DEEP).start()
                load_u(c + DEEP).start()

        return carry

    lax.fori_loop(0, CHUNKS + 4, step, 0)

    for k in range(n_ha):
        own[k] = acc[k * r:(k + 1) * r, :]
        for q in range(4):
            tail[q * r:(q + 1) * r, :] = acc[k * r:(k + 1) * r, q * cols4:(q + 1) * cols4]
        fs[k] = tail[...].astype(BF16)

    def finish(d):
        return remote(fs.at[z ^ d], fr.at[d - 1], t_ss.at[d - 1], t_rs.at[d - 1], me, z ^ d)

    for d in range(1, n_ha):
        finish(d).start()

    for d in range(1, n_wa):
        share_rd(d).wait()
    same, other = rd[...], rd_in[0]
    for d in range(2, n_wa, 2):
        same, other = same + rd_in[d - 1], other + rd_in[d]
    low = jnp.where(core == 0, same, other)
    high = jnp.where(core == 0, other, same)
    xf[0:half, 0:128] = low
    xf[half:rows, 0:128] = high
    for k in range(n_ha):
        rz[k, 0:r, :] = xf[k * r:(k + 1) * r, 0:128]

    def share_rz(d):
        return remote(rz.at[z ^ d], rz_in.at[d - 1], rz_ss.at[d - 1], rz_rs.at[d - 1], me, z ^ d)

    for d in range(1, n_ha):
        share_rz(d).start()
    for d in range(1, n_ha):
        share_rz(d).wait()
    dots = rz[z]
    for d in range(1, n_ha):
        dots = dots + rz_in[d - 1]
    dot = jnp.sum(dots, axis=1, keepdims=True)[0:r]
    inv = inv_own[z][:, 0:1]
    back = inv * inv * dot / D

    for d in range(1, n_ha):
        finish(d).wait()
    own_rows = own[z]
    acc[0:r, :] = own_rows
    for d in range(1, n_ha):
        tail[...] = fr[d - 1].astype(F32)
        for q in range(4):
            acc[0:r, q * cols4:(q + 1) * cols4] += tail[q * r:(q + 1) * r, :]
    scaled = acc[0:r, :] * gain[...]
    out[...] = (go[...].astype(F32) + inv * scaled - res[...].astype(F32) * back).astype(BF16)


def fused_call(n_wa, n_ha, residual_in, grad_out, norm_gain, w_gate, w_up, w_down):
    r, width = residual_in.shape
    rows, half, n_chip = r * n_ha, r * n_ha // 2, n_wa // 2
    ch = w_gate.shape[1] // CHUNKS
    sub = ch // n_chip
    vmem, dma = pltpu.VMEM, pltpu.SemaphoreType.DMA
    inside, outside = pl.BlockSpec(memory_space=pltpu.VMEM), pl.BlockSpec(memory_space=pl.ANY)
    return pl.pallas_call(
        functools.partial(fused, n_wa, n_ha),
        out_shape=jax.ShapeDtypeStruct((r, width), BF16),
        in_specs=[inside] * 3 + [outside] * 3,
        out_specs=inside,
        scratch_shapes=[
            vmem((DEEP, width, ch), BF16), vmem((DEEP, width, ch), BF16), vmem((DEEP_DOWN, ch, width), BF16),
            vmem((n_ha, 4 * r, width // 2), BF16), vmem((4 * r, width // 2), F32),
            vmem((rows, width), F32), vmem((rows, width), F32),
            vmem((rows, width), BF16), vmem((rows, width), BF16),
            vmem((rows, 128), F32), vmem((n_wa - 1, rows, 128), F32),
            vmem((2, half, 128), F32), vmem((n_ha, r, 128), F32),
            vmem((SLOTS, 2, 3 * half, ch), F32), vmem((SLOTS, 3 * half, ch), F32),
            vmem((SLOTS, n_chip, 3 * half, sub), F32), vmem((SLOTS, n_chip - 1, 3 * half, sub), F32),
            vmem((CHUNKS, 2, n_chip, 2 * half, sub), BF16),
            vmem((rows, width), F32),
            vmem((half, 128), F32), vmem((n_wa - 1, half, 128), F32),
            vmem((n_ha, 16, 128), F32), vmem((n_ha - 1, 16, 128), F32),
            vmem((n_ha, r, width), F32),
            vmem((n_ha, 4 * r, width // 4), BF16), vmem((n_ha - 1, 4 * r, width // 4), BF16),
            vmem((4 * r, width // 4), F32),
            dma((DEEP,)), dma((DEEP,)), dma((DEEP_DOWN,)),
            dma((n_ha - 1,)), dma((n_ha - 1,)),
            dma((n_wa - 1,)), dma((n_wa - 1,)),
            dma((SLOTS,)), dma((SLOTS,)),
            dma((SLOTS, n_chip - 1)), dma((SLOTS, n_chip - 1)),
            dma((SLOTS, n_chip - 1)), dma((SLOTS, n_chip - 1)),
            dma((SLOTS,)), dma((SLOTS,)),
            dma((n_wa - 1,)), dma((n_wa - 1,)),
            dma((n_ha - 1,)), dma((n_ha - 1,)),
            dma((n_ha - 1,)), dma((n_ha - 1,)),
        ],
        compiler_params=pltpu.CompilerParams(
            collective_id=0, has_side_effects=True, vmem_limit_bytes=63 * 1024 * 1024
        ),
    )(residual_in, grad_out, norm_gain.astype(F32).reshape(1, width), w_gate, w_up, w_down)


def gate_grads(gate, up, d_hidden):
    sig = jax.nn.sigmoid(gate)
    d_up = (d_hidden * gate * sig).astype(jnp.bfloat16)
    d_gate = (d_hidden * up * sig * (1.0 + gate * (1.0 - sig))).astype(jnp.bfloat16)
    return jnp.stack([d_gate, d_up])


def local(residual_in, grad_out, norm_gain, w_gate, w_up, w_down):
    stream = residual_in.astype(jnp.float32)
    squares = lax.psum(jnp.sum(stream * stream, axis=1), "wa")
    inv_rms = lax.rsqrt(squares / D + 1e-05)[:, None]
    gain_f = norm_gain.astype(jnp.float32)
    normed = (stream * inv_rms * gain_f).astype(jnp.bfloat16)
    stacked = jnp.stack([normed, grad_out])
    piece = lax.all_gather(stacked, "ha", axis=1, tiled=True)
    gate_part = jnp.dot(piece[0], w_gate, preferred_element_type=jnp.float32)
    up_part = jnp.dot(piece[0], w_up, preferred_element_type=jnp.float32)
    back_part = lax.dot_general(
        piece[1], w_down, (((1,), (1,)), ((), ())), preferred_element_type=jnp.float32
    )
    partial_sums = jnp.stack([gate_part, up_part, back_part])
    summed = lax.psum(partial_sums, "wa")
    grads = gate_grads(summed[0], summed[1], summed[2])
    total = lax.dot_general(
        grads[0], w_gate, (((1,), (1,)), ((), ())), preferred_element_type=jnp.float32
    )
    d_normed = lax.psum_scatter(
        total
        + lax.dot_general(
            grads[1], w_up, (((1,), (1,)), ((), ())), preferred_element_type=jnp.float32
        ),
        "ha",
        scatter_dimension=0,
        tiled=True,
    )
    scaled = d_normed * gain_f
    row_dot = lax.psum(jnp.sum(scaled * stream, axis=1), "wa")[:, None]
    grad_in = grad_out.astype(jnp.float32) + inv_rms * scaled - stream * inv_rms**3 * row_dot / D
    return grad_in.astype(jnp.bfloat16)


def fits(mesh, residual_in, w_gate):
    n_wa, n_ha = mesh.shape["wa"], mesh.shape["ha"]
    r, hidden = residual_in.shape[0], w_gate.shape[1]
    powers = all(n >= 2 and n & (n - 1) == 0 for n in (n_wa, n_ha)) and n_wa >= 4
    return (
        powers
        and hidden % (CHUNKS * 128 * (n_wa // 2)) == 0
        and (r * n_ha) % 16 == 0
        and r % 4 == 0
        and r <= 16
    )


def solution(mesh):
    placed = (P("ha", "wa"), P("ha", "wa"), P("wa"), P("wa", "ha"), P("wa", "ha"), P("ha", "wa"))

    def part(*args):
        if fits(mesh, args[0], args[3]):
            return fused_call(mesh.shape["wa"], mesh.shape["ha"], *args)
        return local(*args)

    return jax.shard_map(part, mesh=mesh, in_specs=placed, out_specs=P("ha", "wa"), check_vma=False)
```
